512 devices in a mesh: ctx: 32 (over x, y, core), head: 16 (over z).
Axes of the slice: x: 4, y: 4, z: 16, core: 2. Of those that a mesh axis runs over, the one named last changes fastest.
Arguments:
- queries: bfloat16 [8192, 8192], P(('ctx', 'head')), may hold values from -160 to 160
- image_feats: bfloat16 [4096, 8192], P('ctx', 'head'), may hold values from -6 to 6
- key_value_weight: bfloat16 [8192, 2048], P('head'), may hold values from -0.0625 to 0.0625
- output_gradient: bfloat16 [8192, 8192], P(('ctx', 'head')), may hold values from -6 to 6
- spans: int32 [32, 2], replicated, may hold values from 0 to 8192, as said below
Outputs:
- query_grad: bfloat16 [8192, 8192], P(('ctx', 'head'))
- weight_grad: bfloat16 [8192, 2048], P(('head', 'ctx'))
The draws below stay inside these ranges and needn't reach their ends.
Inputs may be any that keep to these rules, and one draw needn't show every extreme that they name: For image i, 256 * i <= spans[i, 0] < spans[i, 1] <= min(256 * (i + 2), 8192); in every draw some image spans that whole range.
All inputs are finite; a program needn't handle non-finite values.
Results may differ from the reference program's by a relative error of at most 0.029.
The reference program's roundings to bfloat16 on the way count: a program that leaves them out, or rounds other values in their place, can miss the bound.
Values may be sent and summed in bfloat16 or wider, within the bound.
A program may use at most 64 MiB of HBM per device.

```python
import math
import jax
import jax.numpy as jnp
from jax import lax

MODEL_WIDTH = 8192
QUERY_HEADS = 64
KEY_VALUE_HEADS = 8
HEAD_SIZE = 128
TEXT_PER_INDEX = 256
IMAGE_TOKENS = 128
TEXT = 8192
NIMG = 32
IMG_ALL = 4096


def draw_queries(key, part):
    key = jax.random.fold_in(key, 1)
    values = jax.random.truncated_normal(key, -4.0, 4.0, (TEXT, QUERY_HEADS * HEAD_SIZE), jnp.float32)
    return values.astype(jnp.bfloat16)


def draw_spans(key, part):
    key = jax.random.fold_in(key, 7)
    image_ids = jnp.arange(NIMG, dtype=jnp.int32)
    offsets = jax.random.randint(jax.random.fold_in(key, 1), (NIMG,), 0, TEXT_PER_INDEX, dtype=jnp.int32)
    lengths = jax.random.randint(jax.random.fold_in(key, 2), (NIMG,), TEXT_PER_INDEX // 2 + 1, 3 * TEXT_PER_INDEX // 2 + 1, dtype=jnp.int32)
    chosen = jax.random.randint(jax.random.fold_in(key, 3), (), 0, NIMG - 1, dtype=jnp.int32)
    first = image_ids * TEXT_PER_INDEX + offsets
    limit = jnp.minimum((image_ids + 2) * TEXT_PER_INDEX, TEXT)
    last = jnp.minimum(first + lengths, limit)
    first = jnp.where(image_ids == chosen, image_ids * TEXT_PER_INDEX, first)
    last = jnp.where(image_ids == chosen, limit, last)
    first = jnp.where(image_ids == 0, 0, first)
    last = jnp.where(image_ids == NIMG - 1, TEXT, last)
    return jnp.stack([first, last], 1).astype(jnp.int32)


def block_levels(key, shape, split, low, largest):
    factor_of, own = 1.0, jax.random.fold_in(key, 6)
    for dim, blocks in split:
        steps = jnp.exp(jax.random.uniform(jax.random.fold_in(own, dim), (blocks,), jnp.float32, low / len(split), largest / len(split)))
        factor_of = factor_of * jnp.repeat(steps, shape[dim] // blocks).reshape([-1 if axis == dim else 1 for axis in range(len(shape))])
    return factor_of


def noise(stream_key, dims, deviation, most, cuts=(), kind=jnp.bfloat16):
    drawn = jax.random.normal(stream_key, dims, jnp.float32) * deviation
    if len(cuts) > 0:
        drawn = block_levels(stream_key, dims, cuts, -0.22, 0.18) * drawn
    return jnp.clip(drawn, min=-most, max=most).astype(kind)


def setup_inputs(seed: int = 0) -> dict:
    key_of = jax.random.split(jax.random.key(seed), 6)
    return {
        "queries": draw_queries(jax.random.fold_in(key_of[5], 71), 0),
        "image_feats": noise(key_of[1], (IMG_ALL, MODEL_WIDTH), 1.0, 6.0, ((0, 32), (1, 16))),
        "key_value_weight": noise(key_of[2], (MODEL_WIDTH, 2 * KEY_VALUE_HEADS * HEAD_SIZE), MODEL_WIDTH ** -0.5, 0.0625, ((0, 16),)),
        "output_gradient": noise(key_of[3], (TEXT, QUERY_HEADS * HEAD_SIZE), 1.0, 6.0, ((0, 512),)),
        "spans": draw_spans(jax.random.fold_in(key_of[5], 71), 0),
    }


NEG_FILL = -1e+30

def attend_grads(query_rows, grad_rows, key_rows, value_rows, allowed, scaling):
    scores = jnp.einsum('tkgd,skd->kgts', query_rows.astype(jnp.float32), key_rows.astype(jnp.float32)) * scaling
    scores = jnp.where(allowed, scores, NEG_FILL)
    row_max = lax.optimization_barrier(jnp.max(scores, axis=-1, keepdims=True))
    weights = jnp.exp(scores - row_max)
    attn_prob = weights / lax.optimization_barrier(jnp.sum(weights, axis=-1, keepdims=True))
    has_key = jnp.any(allowed, axis=-1)
    attn_prob = jnp.where(has_key[:, None], attn_prob, 0.0)
    prob_low = attn_prob.astype(jnp.bfloat16)
    attended = jnp.einsum('kgts,skd->tkgd', prob_low.astype(jnp.float32), value_rows.astype(jnp.float32))
    row_dot = lax.optimization_barrier(jnp.sum(grad_rows.astype(jnp.float32) * attended, axis=-1))
    grad_prob = jnp.einsum('tkgd,skd->kgts', grad_rows.astype(jnp.float32), value_rows.astype(jnp.float32))
    grad_score = attn_prob * (grad_prob - jnp.transpose(row_dot, (1, 2, 0))[..., None])
    score_low = grad_score.astype(jnp.bfloat16).astype(jnp.float32)
    grad_query = jnp.einsum('kgts,skd->tkgd', score_low, key_rows.astype(jnp.float32)) * scaling
    key_gradient = jnp.einsum('kgts,tkgd->skd', score_low, query_rows.astype(jnp.float32)) * scaling
    value_gradient = jnp.einsum('kgts,tkgd->skd', prob_low.astype(jnp.float32), grad_rows.astype(jnp.float32))
    return (grad_query.astype(jnp.bfloat16), key_gradient, value_gradient)

def reference(queries, image_feats, key_value_weight, output_gradient, spans):
    scaling = 1.0 / math.sqrt(HEAD_SIZE)
    count_of_images = spans.shape[0]
    query_group = QUERY_HEADS // KEY_VALUE_HEADS
    key_value_full = jnp.dot(image_feats, key_value_weight, preferred_element_type=jnp.float32).astype(jnp.bfloat16)
    key_value_full = key_value_full.reshape(count_of_images, IMAGE_TOKENS, KEY_VALUE_HEADS, 2, HEAD_SIZE)
    key_all = key_value_full[:, :, :, 0, :]
    value_all = key_value_full[:, :, :, 1, :]
    empty_block = jnp.zeros((1, IMAGE_TOKENS, KEY_VALUE_HEADS, HEAD_SIZE), jnp.bfloat16)
    key_prev = jnp.concatenate([empty_block, key_all[:-1]], 0)
    value_prev = jnp.concatenate([empty_block, value_all[:-1]], 0)
    query_block_list = queries.reshape(count_of_images, TEXT_PER_INDEX, KEY_VALUE_HEADS, query_group, HEAD_SIZE)
    gradient_blocks = output_gradient.reshape(count_of_images, TEXT_PER_INDEX, KEY_VALUE_HEADS, query_group, HEAD_SIZE)
    shard_ids = jnp.arange(count_of_images, dtype=jnp.int32)

    def one_shard(inputs):
        shard_idx, query_rows, grad_rows, kprev, kown, vprev, vown = inputs
        text_pos = shard_idx * TEXT_PER_INDEX + jnp.arange(TEXT_PER_INDEX, dtype=jnp.int32)
        prev_span = lax.dynamic_index_in_dim(spans, jnp.maximum(shard_idx - 1, 0), 0, keepdims=False)
        own_span = lax.dynamic_index_in_dim(spans, shard_idx, 0, keepdims=False)
        prev_ok = (shard_idx > 0) & (text_pos >= prev_span[0]) & (text_pos < prev_span[1])
        own_ok = (text_pos >= own_span[0]) & (text_pos < own_span[1])
        allowed = jnp.concatenate([jnp.broadcast_to(prev_ok[:, None], (TEXT_PER_INDEX, IMAGE_TOKENS)), jnp.broadcast_to(own_ok[:, None], (TEXT_PER_INDEX, IMAGE_TOKENS))], 1)
        key_rows = jnp.concatenate([kprev, kown], 0)
        value_rows = jnp.concatenate([vprev, vown], 0)
        grad_query, key_gradient, value_gradient = attend_grads(query_rows, grad_rows, key_rows, value_rows, allowed, scaling)
        key_value_gradient = jnp.stack([key_gradient, value_gradient], 2).reshape(2 * IMAGE_TOKENS, KEY_VALUE_HEADS * 2 * HEAD_SIZE)
        return (grad_query.reshape(TEXT_PER_INDEX, QUERY_HEADS * HEAD_SIZE), key_value_gradient)
    grad_q, key_value_gradient = lax.map(one_shard, (shard_ids, query_block_list, gradient_blocks, key_prev, key_all, value_prev, value_all))
    local_portion = key_value_gradient[:, IMAGE_TOKENS:]
    earlier_portion = key_value_gradient[:, :IMAGE_TOKENS]
    later_images = jnp.concatenate([earlier_portion[1:], jnp.zeros((1, IMAGE_TOKENS, KEY_VALUE_HEADS * 2 * HEAD_SIZE), jnp.float32)], 0)
    gradient_key_value = (local_portion + later_images).reshape(count_of_images * IMAGE_TOKENS, KEY_VALUE_HEADS * 2 * HEAD_SIZE).astype(jnp.bfloat16)
    total_tokens = count_of_images * IMAGE_TOKENS
    weight_sum = lax.dot_general(image_feats, gradient_key_value, (((0,), (0,)), ((), ())), preferred_element_type=jnp.float32)
    weight_grad = (weight_sum * (1.0 / math.sqrt(total_tokens))).astype(jnp.bfloat16)
    return (grad_q.reshape(count_of_images * TEXT_PER_INDEX, QUERY_HEADS * HEAD_SIZE), weight_grad)
```

```python
import functools
import math

import jax
import jax.numpy as jnp
from jax import lax
from jax.experimental import pallas as pl
from jax.experimental.pallas import tpu as pltpu
from jax.sharding import PartitionSpec as P

RING = 16
CTX = 32
SIDE = 4
HEADS = 64
KV_HEADS = 8
GROUP = HEADS // KV_HEADS
HEAD_SIZE = 128
TOKENS = 128
ROWS = 16
TEXT_PER_INDEX = 256
HALF = TOKENS // 2
NEG_FILL = -1e30
BF16 = jnp.bfloat16
F32 = jnp.float32


def remote(src, dst, send_sem, recv_sem, device):
    return pltpu.make_async_remote_copy(
        src_ref=src,
        dst_ref=dst,
        send_sem=send_sem,
        recv_sem=recv_sem,
        device_id=device,
        device_id_type=pl.DeviceIdType.MESH,
    )


def matmul(a, b, dims):
    return lax.dot_general(a, b, (dims, ((), ())), preferred_element_type=F32)


def kernel(
    q_hbm, f_hbm, w_hbm, g_hbm, spans,
    qg_hbm, wg_hbm,
    q_ref, f_ref, w_ref, g_ref, qg_ref, wg_ref, ft_ref,
    s1, r1, kv, own, pg_src, pg_dst, s2, r2, kvg,
    c1_src, c1_dst, c1_own, c2_src, c2_dst, c3_src, c3_dst, c3_own,
    in_sem, out_sem, send_sem,
    r1_sem, ag1_sem, prev_sem, pg_sem, r2_sem, ag2_sem, c1_sem, c2_sem, c3_sem,
):
    z = lax.axis_index("head")
    ctx = lax.axis_index("ctx")
    core = lax.rem(ctx, 2)
    chip = ctx // 2
    y = lax.rem(chip, SIDE)
    x = chip // SIDE

    def ring(offset):
        return lax.rem(z + (offset + 2 * RING), RING)

    def at_xy(dx, dy):
        px, py = lax.rem(x + dx, SIDE), lax.rem(y + dy, SIDE)
        return ((px * SIDE + py) * 2 + core, z)

    sides = ((ctx, ring(1)), (ctx, ring(-1)))
    later = (lax.rem(ctx + 1, CTX), z)
    earlier = (lax.rem(ctx + CTX - 1, CTX), z)
    partner = (chip * 2 + (1 - core), z)
    along_x = [at_xy(d, 0) for d in range(1, SIDE)]
    along_y = [at_xy(0, d) for d in range(1, SIDE)]

    loads = [
        pltpu.make_async_copy(src, dst, in_sem.at[n])
        for n, (src, dst) in enumerate(
            ((f_hbm, f_ref), (w_hbm, w_ref), (q_hbm, q_ref), (g_hbm, g_ref))
        )
    ]
    for load in loads:
        load.start()
    barrier = pltpu.get_barrier_semaphore()
    met = (*sides, later, earlier, *along_x, *along_y)
    for device in met:
        pl.semaphore_signal(
            barrier, inc=1, device_id=device, device_id_type=pl.DeviceIdType.MESH
        )
    loads[0].wait()
    loads[1].wait()

    def projected(chunk):
        columns = pl.ds(pl.multiple_of(chunk * HEAD_SIZE, HEAD_SIZE), HEAD_SIZE)
        return matmul(f_ref[...], w_ref[:, columns], ((1,), (0,)))

    halves = (pl.ds(0, HALF), pl.ds(HALF, HALF))

    def send1(way, step, half):
        remote(
            s1.at[way, step, halves[half]], r1.at[way, step, halves[half]],
            send_sem.at[0], r1_sem.at[way, step, half], sides[way],
        ).start()

    def wait1(way, step, half):
        remote(
            s1.at[way, step, halves[half]], r1.at[way, step, halves[half]],
            send_sem.at[0], r1_sem.at[way, step, half], sides[way],
        ).wait_recv()

    first = projected(ring(8))
    s1[0, 0] = first
    s1[1, 0] = first
    pl.semaphore_wait(barrier, len(met))
    send1(0, 0, 0)
    send1(1, 0, 1)
    for step in range(1, 8):
        for way in range(2):
            s1[way, step] = projected(ring(8 - step if way == 0 else 8 + step))
        if step == 1:
            send1(0, 1, 1)
            send1(1, 1, 0)
        for half in range(2):
            for way in range(2):
                if step == 1 and half != way:
                    continue
                wait1(way, step - 1, half)
                s1[way, step, halves[half]] += r1[way, step - 1, halves[half]]
                send1(way, step, half)
    mine = projected(z)
    turned = f_ref[...].astype(F32).T.astype(BF16)
    for n in range(CTX):
        ft_ref[n % 2, pl.ds((n // 2) * ROWS, ROWS), :] = turned[n * ROWS : (n + 1) * ROWS]
    for half in range(2):
        for way in range(2):
            wait1(way, 7, half)
    kv[z, pl.ds(TOKENS, TOKENS)] = (mine + r1[0, 7] + r1[1, 7]).astype(BF16)

    own_rows = pl.ds(TOKENS, TOKENS)
    own_halves = (pl.ds(TOKENS, HALF), pl.ds(TOKENS + HALF, HALF))

    def gather1(way, step):
        owner = ring(-step if way == 0 else step)
        rows = own_rows if step < 7 else own_halves[way]
        block = kv.at[owner, rows]
        return remote(block, block, send_sem.at[1], ag1_sem.at[way, step], sides[way])

    def arrive1(way, step):
        owner = ring(-1 - step if way == 0 else 1 + step)
        rows = own_rows if step < 7 else own_halves[way]
        block = kv.at[owner, rows]
        remote(block, block, send_sem.at[1], ag1_sem.at[way, step], sides[way]).wait_recv()

    def pass_on(chunk):
        return remote(
            kv.at[chunk, own_rows], kv.at[chunk, pl.ds(0, TOKENS)],
            send_sem.at[2], prev_sem.at[chunk], later,
        )

    gather1(0, 0).start()
    gather1(1, 0).start()
    pass_on(z).start()
    loads[2].wait()
    loads[3].wait()

    lane = lax.broadcasted_iota(jnp.int32, (1, TOKENS), 1)
    text_pos = ctx * TEXT_PER_INDEX + z * ROWS + lax.rem(lane, ROWS)
    before = jnp.maximum(ctx - 1, 0)
    prev_ok = (text_pos >= spans[before, 0]) & (text_pos < spans[before, 1]) & (ctx > 0)
    own_ok = (text_pos >= spans[ctx, 0]) & (text_pos < spans[ctx, 1])
    scaling = 1.0 / math.sqrt(HEAD_SIZE)
    is_own = lax.broadcasted_iota(jnp.int32, (2 * TOKENS, TOKENS), 0) >= TOKENS
    allowed = (is_own & own_ok) | (jnp.logical_not(is_own) & prev_ok)

    def stacked(ref, head):
        start = pl.multiple_of(head * (GROUP * HEAD_SIZE), HEAD_SIZE)
        block = ref[:, pl.ds(start, GROUP * HEAD_SIZE)]
        return jnp.concatenate(
            [block[:, n * HEAD_SIZE : (n + 1) * HEAD_SIZE] for n in range(GROUP)], 0
        )

    def attend(head):
        for n in range(2):
            pass_on(2 * head + n).wait_recv()
        keys, values = kv[2 * head], kv[2 * head + 1]
        query, grad = stacked(q_ref, head), stacked(g_ref, head)
        scores = matmul(keys, query, ((1,), (1,))) * scaling
        scores = jnp.where(allowed, scores, NEG_FILL)
        grad_prob = matmul(values, grad, ((1,), (1,)))
        weights = jnp.exp(scores - jnp.max(scores, 0, keepdims=True))
        probs = weights / jnp.sum(weights, 0, keepdims=True)
        probs = jnp.where(allowed, probs, 0.0)
        prob_low = probs.astype(BF16)
        row_dot = jnp.sum(prob_low.astype(F32) * grad_prob, 0, keepdims=True)
        score_low = (probs * (grad_prob - row_dot)).astype(BF16)
        key_grad = matmul(score_low, query, ((1,), (0,))) * scaling
        value_grad = matmul(prob_low, grad, ((1,), (0,)))
        pg_src[2 * head] = key_grad[:TOKENS].astype(BF16)
        pg_src[2 * head + 1] = value_grad[:TOKENS].astype(BF16)
        send_back(head).start()
        own[2 * head] = key_grad[TOKENS:]
        own[2 * head + 1] = value_grad[TOKENS:]
        query_grad = (matmul(score_low, keys, ((0,), (0,))) * scaling).astype(BF16)
        start = pl.multiple_of(head * (GROUP * HEAD_SIZE), HEAD_SIZE)
        qg_ref[:, pl.ds(start, GROUP * HEAD_SIZE)] = jnp.concatenate(
            [query_grad[n * ROWS : (n + 1) * ROWS] for n in range(GROUP)], 1
        )

    def send_back(head):
        pair = pl.ds(2 * head, 2)
        return remote(
            pg_src.at[pair], pg_dst.at[pair], send_sem.at[3], pg_sem.at[head], earlier
        )

    turn = 2 * lax.rem(z, 2) - 1

    def head_at(k):
        offset = ((k + 1) // 2) * (1 if k % 2 else -1)
        return lax.rem(z // 2 + turn * offset + KV_HEADS, KV_HEADS)

    def copy2(way, step):
        rows = halves[way] if step == 0 else pl.ds(0, TOKENS)
        return remote(
            s2.at[way, step, rows], r2.at[way, step, rows],
            send_sem.at[4], r2_sem.at[way, step], sides[way],
        )

    def reduce2(step):
        send_back(head_at(step)).wait_recv()
        if step == 0:
            total = (own[z] + pg_dst[z].astype(F32)).astype(BF16)
            s2[0, 0] = total
            s2[1, 0] = total
            copy2(0, 0).start()
            copy2(1, 0).start()
            return
        for way in range(2):
            chunk = ring(-step if way == 0 else step)
            total = own[chunk] + pg_dst[chunk].astype(F32)
            copy2(way, step - 1).wait_recv()
            if step == 1:
                got = r2[way, 0, halves[way]].astype(F32)
                mixed = total[way * HALF : (way + 1) * HALF] + got
                s2[way, 1, halves[way]] = mixed.astype(BF16)
                rest = 1 - way
                s2[way, 1, halves[rest]] = total[rest * HALF : (rest + 1) * HALF].astype(BF16)
            else:
                s2[way, step] = (total + r2[way, step - 1].astype(F32)).astype(BF16)
            copy2(way, step).start()

    for step in range(8):
        arrive1(0, step)
        arrive1(1, step)
        if step < 7:
            gather1(0, step + 1).start()
            gather1(1, step + 1).start()
            pass_on(ring(-1 - step)).start()
            pass_on(ring(1 + step)).start()
        else:
            pass_on(ring(8)).start()
        attend(head_at(step))
        if step >= 1:
            reduce2(step - 1)
    out_q = pltpu.make_async_copy(qg_ref, qg_hbm, out_sem.at[0])
    out_q.start()
    reduce2(7)
    chunk = ring(8)
    total = own[chunk] + pg_dst[chunk].astype(F32)
    copy2(0, 7).wait_recv()
    copy2(1, 7).wait_recv()
    kvg[chunk] = (total + r2[0, 7].astype(F32) + r2[1, 7].astype(F32)).astype(BF16)

    def gather2(way, step):
        owner = ring(8 - step if way == 0 else 8 + step)
        rows = pl.ds(0, TOKENS) if step < 7 else halves[way]
        block = kvg.at[owner, rows]
        return remote(block, block, send_sem.at[5], ag2_sem.at[way, step], sides[way])

    def arrive2(way, step):
        owner = ring(7 - step if way == 0 else 9 + step)
        rows = pl.ds(0, TOKENS) if step < 7 else halves[way]
        block = kvg.at[owner, rows]
        remote(block, block, send_sem.at[5], ag2_sem.at[way, step], sides[way]).wait_recv()

    def copy_c1(k):
        return remote(c1_src.at[k], c1_dst.at[k], send_sem.at[6], c1_sem.at[k], partner)

    def copies_c2(k):
        found = []
        for d in range(1, SIDE):
            px, py = lax.rem(x + d, SIDE), lax.rem(y + d, SIDE)
            found.append(remote(
                c2_src.at[k, 0, px], c2_dst.at[k, 0, d - 1],
                send_sem.at[7], c2_sem.at[k, 0, d - 1], along_x[d - 1],
            ))
            found.append(remote(
                c2_src.at[k, 1, :, py], c2_dst.at[k, 1, d - 1],
                send_sem.at[7], c2_sem.at[k, 1, d - 1], along_y[d - 1],
            ))
        return found

    def copies_c3(k):
        found = []
        for d in range(1, SIDE):
            px, py = lax.rem(x + d, SIDE), lax.rem(y + d, SIDE)
            found.append(remote(
                c3_src.at[k, 0, py], c3_dst.at[k, 0, d - 1],
                send_sem.at[8], c3_sem.at[k, 0, d - 1], along_y[d - 1],
            ))
            found.append(remote(
                c3_src.at[k, 1, px], c3_dst.at[k, 1, d - 1],
                send_sem.at[8], c3_sem.at[k, 1, d - 1], along_x[d - 1],
            ))
        return found

    def chunks_of(k):
        return ring(8 + k), ring(7 - k)

    def stage1(k):
        a, b = chunks_of(k)
        both = jnp.concatenate([kvg[a], kvg[b]], 1)
        other = matmul(ft_ref[1 - core], both, ((1,), (0,))).astype(BF16)
        for n in range(2):
            part = other[:, n * HEAD_SIZE : (n + 1) * HEAD_SIZE]
            c1_src[k, n] = part.reshape(SIDE, SIDE, ROWS, HEAD_SIZE)
        copy_c1(k).start()
        kept = matmul(ft_ref[core], both, ((1,), (0,)))
        for n in range(2):
            part = kept[:, n * HEAD_SIZE : (n + 1) * HEAD_SIZE]
            c1_own[k, n] = part.reshape(SIDE, SIDE, ROWS, HEAD_SIZE)

    def stage2(k):
        copy_c1(k).wait_recv()
        total = c1_own[k] + c1_dst[k].astype(F32)
        c1_own[k] = total
        c2_src[k] = total.astype(BF16)
        for copy in copies_c2(k):
            copy.start()

    def stage3(k):
        for copy in copies_c2(k):
            copy.wait_recv()
        for n, mine in enumerate((c1_own[k, 0, x], c1_own[k, 1, :, y])):
            total = mine
            for d in range(SIDE - 1):
                total = total + c2_dst[k, n, d].astype(F32)
            c3_own[k, n] = total
            c3_src[k, n] = total.astype(BF16)
        for copy in copies_c3(k):
            copy.start()

    def stage4(k):
        for copy in copies_c3(k):
            copy.wait_recv()
        for n, (mine, chunk) in enumerate(zip((c3_own[k, 0, y], c3_own[k, 1, x]), chunks_of(k))):
            total = mine
            for d in range(SIDE - 1):
                total = total + c3_dst[k, n, d].astype(F32)
            total = total * (1.0 / math.sqrt(CTX * TOKENS))
            columns = pl.ds(pl.multiple_of(chunk * HEAD_SIZE, HEAD_SIZE), HEAD_SIZE)
            wg_ref[:, columns] = total.astype(BF16)

    for step in range(12):
        if 1 <= step <= 8:
            arrive2(0, step - 1)
            arrive2(1, step - 1)
        if step <= 7:
            gather2(0, step).start()
            gather2(1, step).start()
        if 0 <= step - 1 <= 7:
            stage1(step - 1)
        if 0 <= step - 2 <= 7:
            stage2(step - 2)
        if 0 <= step - 3 <= 7:
            stage3(step - 3)
        if 0 <= step - 4 <= 7:
            stage4(step - 4)
    out_w = pltpu.make_async_copy(wg_ref, wg_hbm, out_sem.at[1])
    out_w.start()

    chunks = pl.ds(0, RING - 1)
    sent = (
        s1.reshape(16, TOKENS, HEAD_SIZE).at[chunks],
        kv.at[chunks, pl.ds(0, TOKENS)],
        pg_src,
        pg_src,
        pg_src.at[chunks],
        pg_src.at[chunks],
        c1_src,
        c2_dst,
        c3_dst,
    )
    for n, block in enumerate(sent):
        remote(block, block, send_sem.at[n], in_sem.at[0], later).wait_send()
    out_q.wait()
    out_w.wait()


def per_device(queries, image_feats, key_value_weight, output_gradient, spans):
    anywhere = pl.BlockSpec(memory_space=pl.ANY)
    chunk = (TOKENS, HEAD_SIZE)
    tile = (ROWS, HEAD_SIZE)
    dma = pltpu.SemaphoreType.DMA
    vmem = pltpu.VMEM
    return pl.pallas_call(
        kernel,
        out_shape=(
            jax.ShapeDtypeStruct(queries.shape, BF16),
            jax.ShapeDtypeStruct((ROWS, 2048), BF16),
        ),
        in_specs=[anywhere] * 4 + [pl.BlockSpec(memory_space=pltpu.SMEM)],
        out_specs=(anywhere, anywhere),
        scratch_shapes=[
            vmem(queries.shape, BF16),
            vmem(image_feats.shape, BF16),
            vmem(key_value_weight.shape, BF16),
            vmem(output_gradient.shape, BF16),
            vmem(queries.shape, BF16),
            vmem((ROWS, 2048), BF16),
            vmem((2, 256, TOKENS), BF16),
            vmem((2, 8, *chunk), F32),
            vmem((2, 8, *chunk), F32),
            vmem((RING, 2 * TOKENS, HEAD_SIZE), BF16),
            vmem((RING, *chunk), F32),
            vmem((RING, *chunk), BF16),
            vmem((RING, *chunk), BF16),
            vmem((2, 8, *chunk), BF16),
            vmem((2, 8, *chunk), BF16),
            vmem((RING, *chunk), BF16),
            vmem((8, 2, SIDE, SIDE, *tile), BF16),
            vmem((8, 2, SIDE, SIDE, *tile), BF16),
            vmem((8, 2, SIDE, SIDE, *tile), F32),
            vmem((8, 2, SIDE, SIDE, *tile), BF16),
            vmem((8, 2, SIDE - 1, SIDE, *tile), BF16),
            vmem((8, 2, SIDE, *tile), BF16),
            vmem((8, 2, SIDE - 1, *tile), BF16),
            vmem((8, 2, SIDE, *tile), F32),
            dma((4,)),
            dma((2,)),
            dma((9,)),
            dma((2, 8, 2)),
            dma((2, 8)),
            dma((RING,)),
            dma((KV_HEADS,)),
            dma((2, 8)),
            dma((2, 8)),
            dma((8,)),
            dma((8, 2, 3)),
            dma((8, 2, 3)),
        ],
        compiler_params=pltpu.CompilerParams(
            collective_id=0, has_side_effects=True, vmem_limit_bytes=40 * 1024 * 1024
        ),
    )(queries, image_feats, key_value_weight, output_gradient, spans)


def solution(mesh):
    return jax.shard_map(
        per_device,
        mesh=mesh,
        in_specs=(
            P(("ctx", "head"), None),
            P("ctx", "head"),
            P("head", None),
            P(("ctx", "head"), None),
            P(),
        ),
        out_specs=(P(("ctx", "head"), None), P(("head", "ctx"), None)),
        check_vma=False,
    )
```

```python
import math

import jax
import jax.numpy as jnp
from jax import lax
from jax.experimental import pallas as pl
from jax.experimental.pallas import tpu as pltpu
from jax.sharding import PartitionSpec as P

RING = 16
CTX = 32
SIDE = 4
CHIPS = SIDE * SIDE
HEAD_SIZE = 128
KV_HEADS = 8
GROUP = 8
WIDE = GROUP * HEAD_SIZE
TOKENS = 128
ROWS = 16
TEXT_PER_INDEX = 256
HALF = TOKENS // 2
NEG_FILL = -1e30
BF16 = jnp.bfloat16
F32 = jnp.float32

SPREAD = {3: 0, 1: 0, 6: 3, 4: 3, 2: 3, 8: 6, 7: 6, 5: 6}
GATHER = {3: 0, 1: 0, 6: 3, 4: 3, 2: 3, 8: 6, 7: 6, 5: 6}
GATHER_INNER = (6, 3)


def children(tree, place):
    return [q for q, p in tree.items() if p == place]


def remote(src, dst, send_sem, recv_sem, device):
    return pltpu.make_async_remote_copy(
        src_ref=src,
        dst_ref=dst,
        send_sem=send_sem,
        recv_sem=recv_sem,
        device_id=device,
        device_id_type=pl.DeviceIdType.MESH,
    )


def matmul(a, b, dims):
    return lax.dot_general(a, b, (dims, ((), ())), preferred_element_type=F32)


def kernel(
    q_hbm, f_hbm, w_hbm, g_hbm, spans_hbm,
    qg_hbm, wg_hbm,
    spans, f_ref, w_ref, q_ref, g_ref, qg_ref, wg_ref, ft_src, ft_ref,
    part, r1, kv, own, pg_src, pg_dst, s2, r2, kvg,
    c2_own, c2_src, c2_dst,
    in_sem, out_sem, send_sem,
    ft_sem, r1_sem, ag1_sem, prev_sem, pg_sem, r2_sem, ag2_sem, c1_sem, c2_sem,
):
    z = lax.axis_index("head")
    ctx = lax.axis_index("ctx")
    core = lax.rem(ctx, 2)
    chip = ctx // 2
    y = lax.rem(chip, SIDE)
    x = chip // SIDE

    def ring(offset):
        return lax.rem(z + (offset + 2 * RING), RING)

    def chip_at(n):
        return lax.rem(x + n // SIDE, SIDE) * SIDE + lax.rem(y + n % SIDE, SIDE)

    later = (lax.rem(ctx + 1, CTX), z)
    earlier = (lax.rem(ctx + CTX - 1, CTX), z)
    partner = (chip * 2 + (1 - core), z)

    loads = [
        pltpu.make_async_copy(src, dst, in_sem.at[n])
        for n, (src, dst) in enumerate(
            ((f_hbm, f_ref), (w_hbm, w_ref), (q_hbm, q_ref), (g_hbm, g_ref), (spans_hbm, spans))
        )
    ]
    for load in loads:
        load.start()
    barrier = pltpu.get_barrier_semaphore()
    met = [(ctx, ring(d)) for d in (1, 2, 3, -1, -2, -3)] + [later, earlier]
    met += [(chip_at(n) * 2 + core, z) for n in range(1, CHIPS)]
    for device in met:
        pl.semaphore_signal(
            barrier, inc=1, device_id=device, device_id_type=pl.DeviceIdType.MESH
        )
    loads[0].wait()
    loads[1].wait()
    both_sides = (0, 1)
    halves = (pl.ds(0, HALF), pl.ds(HALF, HALF))
    whole = pl.ds(0, TOKENS)

    def rows_at(side, place):
        return halves[side] if place == 8 else whole

    def project(chunk):
        columns = pl.ds(pl.multiple_of(chunk * HEAD_SIZE, HEAD_SIZE), HEAD_SIZE)
        part[chunk] = matmul(f_ref[...], w_ref[:, columns], ((1,), (0,)))

    def up1(side, place, half):
        way = 1 - 2 * side
        owner = ring(-way * place)
        target = ring(-way * (place - GATHER[place]))
        return remote(
            part.at[owner, halves[half]], r1.at[side, place - 1, halves[half]],
            send_sem.at[0], r1_sem.at[side, place - 1, half], (ctx, target),
        )

    def send1(half, *places):
        for place in places:
            for side in both_sides:
                if place < 8 or side == half:
                    up1(side, place, half).start()

    def sum1(half, place):
        for side in both_sides:
            way = 1 - 2 * side
            owner = ring(-way * place)
            for q in children(GATHER, place):
                if q < 8 or side == half:
                    up1(side, q, half).wait_recv()
                    part[owner, halves[half]] += r1[side, q - 1, halves[half]]
            up1(side, place, half).start()

    project(ring(8))
    pl.semaphore_wait(barrier, len(met))
    send1(0, 8)
    for place in (7, 5):
        for side in both_sides:
            project(ring(place if side else -place))
        send1(0, place)
    send1(1, 8, 7, 5)
    for place in (6, 4, 2, 3, 1, 0):
        for side in both_sides:
            if place > 0 or side == 0:
                project(ring(place if side else -place))
    turned = f_ref[...].astype(F32).T.astype(BF16)
    image_lanes = pl.ds(pl.multiple_of(core * TOKENS, TOKENS), TOKENS)
    for n in range(CTX):
        ft_src[n % 2, pl.ds((n // 2) * ROWS, ROWS), :] = turned[n * ROWS : (n + 1) * ROWS]
    ft_ref[:, image_lanes] = ft_src[core]
    features = remote(
        ft_src.at[1 - core], ft_ref.at[:, image_lanes], send_sem.at[1], ft_sem.at[0], partner
    )
    features.start()
    sum1(0, 6)
    sum1(1, 6)
    send1(0, 4, 2)
    send1(1, 4, 2)
    sum1(0, 3)
    sum1(1, 3)
    send1(0, 1)
    send1(1, 1)

    own_rows, prev_rows = pl.ds(TOKENS, TOKENS), pl.ds(0, TOKENS)
    for half in range(2):
        total = part[z, halves[half]]
        for q in children(GATHER, 0):
            for side in both_sides:
                up1(side, q, half).wait_recv()
                total = total + r1[side, q - 1, halves[half]]
        kv[z, pl.ds(TOKENS + half * HALF, HALF)] = total.astype(BF16)

    def spread1(side, place, child, half):
        way = 1 - 2 * side
        block = kv.at[ring(-way * place), pl.ds(TOKENS + half * HALF, HALF)]
        target = ring(way * (child - place))
        return remote(
            block, block, send_sem.at[2], ag1_sem.at[side, child - 1, half], (ctx, target)
        )

    def forward1(side, place, half):
        for child in children(SPREAD, place):
            if child < 8 or side == half:
                spread1(side, place, child, half).start()

    def pass_on(chunk):
        return remote(
            kv.at[chunk, own_rows], kv.at[chunk, prev_rows],
            send_sem.at[3], prev_sem.at[chunk], later,
        )

    def take1(*places):
        for place in places:
            for half in range(2):
                for side in both_sides:
                    if place < 8 or side == half:
                        spread1(side, place, place, half).wait_recv()
                        forward1(side, place, half)
            for side in both_sides[: 1 if place == 8 else 2]:
                pass_on(ring(place if side else -place)).start()

    for half in range(2):
        for side in both_sides:
            forward1(side, 0, half)
    pass_on(z).start()
    loads[2].wait()
    loads[3].wait()
    loads[4].wait()

    lane = lax.broadcasted_iota(jnp.int32, (1, TOKENS), 1)
    token = ctx * TEXT_PER_INDEX + z * ROWS + lax.rem(lane, ROWS)
    before = jnp.maximum(ctx - 1, 0)
    prev_ok = (token >= spans[0, before]) & (token < spans[1, before]) & (ctx > 0)
    own_ok = (token >= spans[0, ctx]) & (token < spans[1, ctx])
    is_own = lax.broadcasted_iota(jnp.int32, (2 * TOKENS, TOKENS), 0) >= TOKENS
    allowed = (is_own & own_ok) | (jnp.logical_not(is_own) & prev_ok)
    scaling = 1.0 / math.sqrt(HEAD_SIZE)

    def stacked(ref, head):
        block = ref[:, pl.ds(pl.multiple_of(head * WIDE, WIDE), WIDE)]
        return jnp.concatenate(
            [block[:, n * HEAD_SIZE : (n + 1) * HEAD_SIZE] for n in range(GROUP)], 0
        )

    def attend(head):
        for n in range(2):
            pass_on(2 * head + n).wait_recv()
        keys, values = kv[2 * head], kv[2 * head + 1]
        query, grad = stacked(q_ref, head), stacked(g_ref, head)
        scores = matmul(keys, query, ((1,), (1,))) * scaling
        scores = jnp.where(allowed, scores, NEG_FILL)
        grad_prob = matmul(values, grad, ((1,), (1,)))
        weights = jnp.exp(scores - jnp.max(scores, 0, keepdims=True))
        probs = weights * (1.0 / jnp.sum(weights, 0, keepdims=True))
        probs = jnp.where(allowed, probs, 0.0)
        prob_low = probs.astype(BF16)
        row_dot = jnp.sum(prob_low.astype(F32) * grad_prob, 0, keepdims=True)
        score_low = (probs * (grad_prob - row_dot)).astype(BF16)
        key_grad = matmul(score_low, query, ((1,), (0,))) * scaling
        value_grad = matmul(prob_low, grad, ((1,), (0,)))
        pg_src[2 * head] = key_grad[:TOKENS].astype(BF16)
        pg_src[2 * head + 1] = value_grad[:TOKENS].astype(BF16)
        send_back(head).start()
        own[2 * head] = key_grad[TOKENS:]
        own[2 * head + 1] = value_grad[TOKENS:]
        query_grad = (matmul(score_low, keys, ((0,), (0,))) * scaling).astype(BF16)
        qg_ref[:, pl.ds(pl.multiple_of(head * WIDE, WIDE), WIDE)] = jnp.concatenate(
            [query_grad[n * ROWS : (n + 1) * ROWS] for n in range(GROUP)], 1
        )

    def send_back(head):
        pair = pl.ds(2 * head, 2)
        return remote(
            pg_src.at[pair], pg_dst.at[pair], send_sem.at[4], pg_sem.at[head], earlier
        )

    turn = 2 * lax.rem(z, 2) - 1

    def head_at(k):
        offset = ((k + 1) // 2) * (1 if k % 2 else -1)
        return lax.rem(z // 2 + turn * offset + KV_HEADS, KV_HEADS)

    def up2(side, place):
        way = 1 - 2 * side
        rows = rows_at(side, place)
        target = ring(-way * (place - GATHER[place]))
        return remote(
            s2.at[side, place - 1, rows], r2.at[side, place - 1, rows],
            send_sem.at[5], r2_sem.at[side, place - 1], (ctx, target),
        )

    def gathered(chunk):
        return own[chunk] + pg_dst[chunk].astype(F32)

    def leaf2(k):
        send_back(head_at(k)).wait_recv()
        place = 8 - k
        if place in GATHER_INNER:
            return
        for side in both_sides:
            way = 1 - 2 * side
            s2[side, place - 1] = gathered(ring(8 - way * place)).astype(BF16)
            up2(side, place).start()

    def inner2(place):
        for side in both_sides:
            way = 1 - 2 * side
            total = gathered(ring(8 - way * place))
            for q in children(GATHER, place):
                up2(side, q).wait_recv()
                if q == 8:
                    got = r2[side, 7, halves[side]].astype(F32)
                    mixed = total[side * HALF : (side + 1) * HALF] + got
                    rest = total[(1 - side) * HALF : (2 - side) * HALF]
                    total = jnp.concatenate([rest, mixed] if side else [mixed, rest], 0)
                else:
                    total = total + r2[side, q - 1].astype(F32)
            s2[side, place - 1] = total.astype(BF16)
            up2(side, place).start()

    take1(3, 1)
    attend(head_at(0))
    take1(6, 4, 2)
    leaf2(0)
    for k in (1, 2, 3):
        attend(head_at(k))
    take1(7, 5, 8)
    for k in (1, 2, 3):
        leaf2(k)
    for k in (4, 5, 6):
        attend(head_at(k))
    inner2(6)
    attend(head_at(7))
    out_q = pltpu.make_async_copy(qg_ref, qg_hbm, out_sem.at[0])
    out_q.start()
    for k in (4, 5, 6, 7):
        leaf2(k)
    inner2(3)
    total = gathered(ring(8))
    for q in children(GATHER, 0):
        for side in both_sides:
            up2(side, q).wait_recv()
            total = total + r2[side, q - 1].astype(F32)
    image_rows = pl.ds(pl.multiple_of(core * TOKENS, TOKENS), TOKENS)
    kvg[z, image_rows] = total.astype(BF16)

    def spread2(side, place, child, half):
        way = 1 - 2 * side
        start = pl.multiple_of(core * TOKENS + half * HALF, HALF)
        block = kvg.at[ring(-way * place), pl.ds(start, HALF)]
        target = ring(way * (child - place))
        return remote(
            block, block, send_sem.at[6], ag2_sem.at[side, child - 1, half], (ctx, target)
        )

    def forward2(side, place, half):
        for child in children(SPREAD, place):
            if child < 8 or side == half:
                spread2(side, place, child, half).start()

    def share(owner):
        block = kvg.at[owner, image_rows]
        return remote(block, block, send_sem.at[7], c1_sem.at[owner], partner)

    def shared(owner):
        block = kvg.at[owner, pl.ds(pl.multiple_of((1 - core) * TOKENS, TOKENS), TOKENS)]
        remote(block, block, send_sem.at[7], c1_sem.at[owner], partner).wait_recv()

    def take2(*places):
        for place in places:
            for half in range(2):
                for side in both_sides:
                    if place < 8 or side == half:
                        spread2(side, place, place, half).wait_recv()
                        forward2(side, place, half)
            for side in both_sides[: 1 if place == 8 else 2]:
                share(ring(place if side else -place)).start()

    def owners_of(place):
        return (z, ring(8)) if place == 8 else (ring(-place), ring(place))

    def copies_c2(k):
        return [
            remote(
                c2_src.at[k, chip_at(n)], c2_dst.at[k, n - 1],
                send_sem.at[8], c2_sem.at[k, n - 1], (chip_at(n) * 2 + core, z),
            )
            for n in range(1, CHIPS)
        ]

    def multiply(*places):
        for place in places:
            k = place - 1
            owners = owners_of(place)
            for owner in owners:
                shared(owner)
            product = matmul(
                ft_ref[...], jnp.concatenate([kvg[n] for n in owners], 1), ((1,), (0,))
            )
            c2_own[k] = product
            c2_src[k] = product.astype(BF16).reshape(CHIPS, ROWS, 2 * HEAD_SIZE)
            for copy in copies_c2(k):
                copy.start()

    def finish(place):
        k = place - 1
        total = c2_own[k, pl.ds(pl.multiple_of(chip * ROWS, ROWS), ROWS)]
        for n, copy in enumerate(copies_c2(k)):
            copy.wait_recv()
            total = total + c2_dst[k, n].astype(F32)
        total = (total * (1.0 / math.sqrt(CTX * TOKENS))).astype(BF16)
        for n, owner in enumerate(owners_of(place)):
            chunk = lax.rem(owner + 8, RING)
            columns = pl.ds(pl.multiple_of(chunk * HEAD_SIZE, HEAD_SIZE), HEAD_SIZE)
            wg_ref[:, columns] = total[:, n * HEAD_SIZE : (n + 1) * HEAD_SIZE]

    for half in range(2):
        for side in both_sides:
            forward2(side, 0, half)
    share(z).start()
    features.wait_recv()
    take2(3, 1)
    multiply(1, 3)
    take2(6, 4, 2)
    multiply(2, 4, 6)
    take2(7, 5)
    multiply(5, 7)
    take2(8)
    multiply(8)
    for place in (1, 3, 2, 4, 6, 5, 7, 8):
        finish(place)
    out_w = pltpu.make_async_copy(wg_ref, wg_hbm, out_sem.at[1])
    out_w.start()

    fifteen = pl.ds(0, RING - 1)
    sent = (
        part.at[fifteen],
        ft_src.at[0],
        pg_src.at[fifteen],
        pg_src,
        pg_src,
        pg_src.at[fifteen],
        pg_src.at[fifteen],
        pg_src,
        c2_dst,
    )
    for n, block in enumerate(sent):
        remote(block, block, send_sem.at[n], in_sem.at[0], partner).wait_send()
    out_q.wait()
    out_w.wait()


def settle(a_in, b_in, a_out, b_out):
    a_out[...] = a_in[...]
    b_out[...] = b_in[...]


def per_device(queries, image_feats, key_value_weight, output_gradient, spans):
    anywhere = pl.BlockSpec(memory_space=pl.ANY)
    chunk = (TOKENS, HEAD_SIZE)
    double = (2 * TOKENS, HEAD_SIZE)
    dma = pltpu.SemaphoreType.DMA
    vmem = pltpu.VMEM
    results = pl.pallas_call(
        kernel,
        out_shape=(
            jax.ShapeDtypeStruct(queries.shape, BF16),
            jax.ShapeDtypeStruct((ROWS, 2048), BF16),
        ),
        in_specs=[anywhere] * 5,
        out_specs=(anywhere, anywhere),
        scratch_shapes=[
            pltpu.SMEM((2, CTX), jnp.int32),
            vmem(image_feats.shape, BF16),
            vmem(key_value_weight.shape, BF16),
            vmem(queries.shape, BF16),
            vmem(output_gradient.shape, BF16),
            vmem(queries.shape, BF16),
            vmem((ROWS, 2048), BF16),
            vmem((2, 256, TOKENS), BF16),
            vmem((256, 2 * TOKENS), BF16),
            vmem((RING, *chunk), F32),
            vmem((2, 8, *chunk), F32),
            vmem((RING, *double), BF16),
            vmem((RING, *chunk), F32),
            vmem((RING, *chunk), BF16),
            vmem((RING, *chunk), BF16),
            vmem((2, 8, *chunk), BF16),
            vmem((2, 8, *chunk), BF16),
            vmem((RING, *double), BF16),
            vmem((8, 256, 2 * HEAD_SIZE), F32),
            vmem((8, CHIPS, ROWS, 2 * HEAD_SIZE), BF16),
            vmem((8, CHIPS - 1, ROWS, 2 * HEAD_SIZE), BF16),
            dma((5,)),
            dma((2,)),
            dma((9,)),
            dma((1,)),
            dma((2, 8, 2)),
            dma((2, 8, 2)),
            dma((RING,)),
            dma((KV_HEADS,)),
            dma((2, 8)),
            dma((2, 8, 2)),
            dma((RING,)),
            dma((8, CHIPS - 1)),
        ],
        compiler_params=pltpu.CompilerParams(
            collective_id=0, has_side_effects=True, vmem_limit_bytes=60 * 1024 * 1024
        ),
    )(queries, image_feats, key_value_weight, output_gradient, spans.T)
    inside = pl.BlockSpec(memory_space=pltpu.VMEM)
    return pl.pallas_call(
        settle,
        out_shape=tuple(jax.ShapeDtypeStruct(r.shape, r.dtype) for r in results),
        in_specs=[inside] * 2,
        out_specs=(inside, inside),
    )(*results)


def solution(mesh):
    return jax.shard_map(
        per_device,
        mesh=mesh,
        in_specs=(
            P(("ctx", "head"), None),
            P("ctx", "head"),
            P("head", None),
            P(("ctx", "head"), None),
            P(),
        ),
        out_specs=(P(("ctx", "head"), None), P(("head", "ctx"), None)),
        check_vma=False,
    )
```

```python
import math

import jax
import jax.numpy as jnp
from jax import lax
from jax.experimental import pallas as pl
from jax.experimental.pallas import tpu as pltpu
from jax.sharding import PartitionSpec as P

RING = 16
CTX = 32
SIDE = 4
CHIPS = SIDE * SIDE
HEAD_SIZE = 128
KV_HEADS = 8
GROUP = 8
WIDE = GROUP * HEAD_SIZE
TOKENS = 128
ROWS = 16
TEXT_PER_INDEX = 256
HALF = TOKENS // 2
NEG_FILL = -1e30
BF16 = jnp.bfloat16
F32 = jnp.float32

SPREAD = {3: 0, 2: 0, 1: 0, 6: 3, 5: 3, 4: 3, 8: 6, 7: 6}
GATHER = {3: 0, 2: 0, 1: 0, 6: 3, 5: 3, 4: 3, 8: 6, 7: 6}
PROJECT = {3: 0, 1: 0, 6: 3, 4: 3, 2: 3, 8: 6, 7: 6, 5: 6}
GATHER_INNER = (6, 3)


def children(tree, place):
    return [q for q, p in tree.items() if p == place]


def remote(src, dst, send_sem, recv_sem, device):
    return pltpu.make_async_remote_copy(
        src_ref=src,
        dst_ref=dst,
        send_sem=send_sem,
        recv_sem=recv_sem,
        device_id=device,
        device_id_type=pl.DeviceIdType.MESH,
    )


def matmul(a, b, dims):
    return lax.dot_general(a, b, (dims, ((), ())), preferred_element_type=F32)


def kernel(
    q_hbm, f_hbm, w_hbm, g_hbm, spans_hbm,
    qg_hbm, wg_hbm,
    spans, f_ref, w_ref, q_ref, g_ref, qg_ref, wg_ref, ft_src, ft_ref,
    part, r1, kv, own, pg_src, pg_dst, s2, r2, kvg,
    c2_own, c2_src, c2_dst,
    in_sem, out_sem, send_sem,
    ft_sem, r1_sem, ag1_sem, prev_sem, pg_sem, r2_sem, ag2_sem, c1_sem, c2_sem,
):
    z = lax.axis_index("head")
    ctx = lax.axis_index("ctx")
    core = lax.rem(ctx, 2)
    chip = ctx // 2
    y = lax.rem(chip, SIDE)
    x = chip // SIDE

    def ring(offset):
        return lax.rem(z + (offset + 2 * RING), RING)

    def chip_at(n):
        return lax.rem(x + n // SIDE, SIDE) * SIDE + lax.rem(y + n % SIDE, SIDE)

    later = (lax.rem(ctx + 1, CTX), z)
    earlier = (lax.rem(ctx + CTX - 1, CTX), z)
    partner = (chip * 2 + (1 - core), z)

    loads = [
        pltpu.make_async_copy(src, dst, in_sem.at[n])
        for n, (src, dst) in enumerate(
            ((f_hbm, f_ref), (w_hbm, w_ref), (q_hbm, q_ref), (g_hbm, g_ref), (spans_hbm, spans))
        )
    ]
    for load in loads:
        load.start()
    barrier = pltpu.get_barrier_semaphore()
    met = [(ctx, ring(d)) for d in (1, 2, 3, -1, -2, -3)] + [later, earlier]
    met += [(chip_at(n) * 2 + core, z) for n in range(1, CHIPS)]
    for device in met:
        pl.semaphore_signal(
            barrier, inc=1, device_id=device, device_id_type=pl.DeviceIdType.MESH
        )
    loads[0].wait()
    loads[1].wait()
    both_sides = (0, 1)
    halves = (pl.ds(0, HALF), pl.ds(HALF, HALF))

    def project(chunk):
        columns = pl.ds(pl.multiple_of(chunk * HEAD_SIZE, HEAD_SIZE), HEAD_SIZE)
        part[chunk] = matmul(f_ref[...], w_ref[:, columns], ((1,), (0,)))

    def up1(side, place, half):
        way = 1 - 2 * side
        owner = ring(-way * place)
        target = ring(-way * (place - PROJECT[place]))
        return remote(
            part.at[owner, halves[half]], r1.at[side, place - 1, halves[half]],
            send_sem.at[0], r1_sem.at[side, place - 1, half], (ctx, target),
        )

    def send1(half, *places):
        for place in places:
            for side in both_sides:
                if place < 8 or side == half:
                    up1(side, place, half).start()

    def sum1(half, place):
        for side in both_sides:
            way = 1 - 2 * side
            owner = ring(-way * place)
            for q in children(PROJECT, place):
                if q < 8 or side == half:
                    up1(side, q, half).wait_recv()
                    part[owner, halves[half]] += r1[side, q - 1, halves[half]]
            up1(side, place, half).start()

    project(ring(8))
    pl.semaphore_wait(barrier, len(met))
    send1(0, 8)
    for place in (7, 5):
        for side in both_sides:
            project(ring(place if side else -place))
        send1(0, place)
    send1(1, 8, 7, 5)
    for place in (6, 4, 2, 3, 1, 0):
        for side in both_sides:
            if place > 0 or side == 0:
                project(ring(place if side else -place))
    turned = f_ref[...].astype(F32).T.astype(BF16)
    image_lanes = pl.ds(pl.multiple_of(core * TOKENS, TOKENS), TOKENS)
    for n in range(CTX):
        ft_src[n % 2, pl.ds((n // 2) * ROWS, ROWS), :] = turned[n * ROWS : (n + 1) * ROWS]
    ft_ref[:, image_lanes] = ft_src[core]
    features = remote(
        ft_src.at[1 - core], ft_ref.at[:, image_lanes], send_sem.at[1], ft_sem.at[0], partner
    )
    features.start()
    sum1(0, 6)
    sum1(1, 6)
    send1(0, 4, 2)
    send1(1, 4, 2)
    sum1(0, 3)
    sum1(1, 3)
    send1(0, 1)
    send1(1, 1)

    own_rows, prev_rows = pl.ds(TOKENS, TOKENS), pl.ds(0, TOKENS)

    def spread1(side, place, child, half):
        way = 1 - 2 * side
        block = kv.at[ring(-way * place), pl.ds(TOKENS + half * HALF, HALF)]
        target = ring(way * (child - place))
        return remote(
            block, block, send_sem.at[2], ag1_sem.at[side, child - 1, half], (ctx, target)
        )

    def forward1(side, place, half):
        for child in children(SPREAD, place):
            if child < 8 or side == half:
                spread1(side, place, child, half).start()

    def pass_on(chunk):
        return remote(
            kv.at[chunk, own_rows], kv.at[chunk, prev_rows],
            send_sem.at[3], prev_sem.at[chunk], later,
        )

    def take1(*places):
        for place in places:
            for half in range(2):
                for side in both_sides:
                    if place < 8 or side == half:
                        spread1(side, place, place, half).wait_recv()
                        forward1(side, place, half)
            for side in both_sides[: 1 if place == 8 else 2]:
                pass_on(ring(place if side else -place)).start()

    for half in range(2):
        total = part[z, halves[half]]
        for q in children(PROJECT, 0):
            for side in both_sides:
                up1(side, q, half).wait_recv()
                total = total + r1[side, q - 1, halves[half]]
        kv[z, pl.ds(TOKENS + half * HALF, HALF)] = total.astype(BF16)
        for side in both_sides:
            forward1(side, 0, half)
    pass_on(z).start()
    loads[2].wait()
    loads[3].wait()
    loads[4].wait()

    lane = lax.broadcasted_iota(jnp.int32, (1, TOKENS), 1)
    token = ctx * TEXT_PER_INDEX + z * ROWS + lax.rem(lane, ROWS)
    before = jnp.maximum(ctx - 1, 0)
    prev_ok = (token >= spans[0, before]) & (token < spans[1, before]) & (ctx > 0)
    own_ok = (token >= spans[0, ctx]) & (token < spans[1, ctx])
    is_own = lax.broadcasted_iota(jnp.int32, (2 * TOKENS, TOKENS), 0) >= TOKENS
    allowed = (is_own & own_ok) | (jnp.logical_not(is_own) & prev_ok)
    scaling = 1.0 / math.sqrt(HEAD_SIZE)

    def stacked(ref, head):
        block = ref[:, pl.ds(pl.multiple_of(head * WIDE, WIDE), WIDE)]
        return jnp.concatenate(
            [block[:, n * HEAD_SIZE : (n + 1) * HEAD_SIZE] for n in range(GROUP)], 0
        )

    def attend(head):
        for n in range(2):
            pass_on(2 * head + n).wait_recv()
        keys, values = kv[2 * head], kv[2 * head + 1]
        query, grad = stacked(q_ref, head), stacked(g_ref, head)
        scores = matmul(keys, query, ((1,), (1,))) * scaling
        scores = jnp.where(allowed, scores, NEG_FILL)
        grad_prob = matmul(values, grad, ((1,), (1,)))
        weights = jnp.exp(scores - jnp.max(scores, 0, keepdims=True))
        probs = weights * (1.0 / jnp.sum(weights, 0, keepdims=True))
        probs = jnp.where(allowed, probs, 0.0)
        prob_low = probs.astype(BF16)
        row_dot = jnp.sum(prob_low.astype(F32) * grad_prob, 0, keepdims=True)
        score_low = (probs * (grad_prob - row_dot)).astype(BF16)
        key_grad = matmul(score_low, query, ((1,), (0,))) * scaling
        value_grad = matmul(prob_low, grad, ((1,), (0,)))
        pg_src[2 * head] = key_grad[:TOKENS].astype(BF16)
        pg_src[2 * head + 1] = value_grad[:TOKENS].astype(BF16)
        send_back(head).start()
        own[2 * head] = key_grad[TOKENS:]
        own[2 * head + 1] = value_grad[TOKENS:]
        query_grad = (matmul(score_low, keys, ((0,), (0,))) * scaling).astype(BF16)
        qg_ref[:, pl.ds(pl.multiple_of(head * WIDE, WIDE), WIDE)] = jnp.concatenate(
            [query_grad[n * ROWS : (n + 1) * ROWS] for n in range(GROUP)], 1
        )

    def send_back(head):
        pair = pl.ds(2 * head, 2)
        return remote(
            pg_src.at[pair], pg_dst.at[pair], send_sem.at[4], pg_sem.at[head], earlier
        )

    turn = 2 * lax.rem(z, 2) - 1

    def head_at(k):
        offset = ((k + 1) // 2) * (1 if k % 2 else -1)
        return lax.rem(z // 2 + turn * offset + KV_HEADS, KV_HEADS)

    def up2(side, place, half):
        way = 1 - 2 * side
        target = ring(-way * (place - GATHER[place]))
        return remote(
            s2.at[side, place - 1, halves[half]], r2.at[side, place - 1, halves[half]],
            send_sem.at[5], r2_sem.at[side, place - 1, half], (ctx, target),
        )

    def gathered(chunk, half):
        return own[chunk, halves[half]] + pg_dst[chunk, halves[half]].astype(F32)

    def summed(side, place, half, total):
        for q in children(GATHER, place):
            if q < 8 or side == half:
                up2(side, q, half).wait_recv()
                total = total + r2[side, q - 1, halves[half]].astype(F32)
        return total

    def send2(place):
        for half in range(2):
            for side in both_sides:
                if place < 8 or side == half:
                    way = 1 - 2 * side
                    total = summed(side, place, half, gathered(ring(8 - way * place), half))
                    s2[side, place - 1, halves[half]] = total.astype(BF16)
                    up2(side, place, half).start()

    def leaf2(k):
        send_back(head_at(k)).wait_recv()
        if 8 - k not in GATHER_INNER:
            send2(8 - k)

    take1(3, 2, 1)
    for k in (0, 1, 2):
        attend(head_at(k))
    take1(6, 5, 4)
    for k in (0, 1, 2):
        leaf2(k)
    for k in (3, 4, 5):
        attend(head_at(k))
    take1(8, 7)
    send2(6)
    for k in (3, 4):
        leaf2(k)
    for k in (6, 7):
        attend(head_at(k))
    out_q = pltpu.make_async_copy(qg_ref, qg_hbm, out_sem.at[0])
    out_q.start()
    for k in (5, 6, 7):
        leaf2(k)
    send2(3)
    image_rows = pl.ds(pl.multiple_of(core * TOKENS, TOKENS), TOKENS)

    def spread2(side, place, child, half):
        way = 1 - 2 * side
        start = pl.multiple_of(core * TOKENS + half * HALF, HALF)
        block = kvg.at[ring(-way * place), pl.ds(start, HALF)]
        target = ring(way * (child - place))
        return remote(
            block, block, send_sem.at[6], ag2_sem.at[side, child - 1, half], (ctx, target)
        )

    def forward2(side, place, half):
        for child in children(SPREAD, place):
            if child < 8 or side == half:
                spread2(side, place, child, half).start()

    def share(owner):
        block = kvg.at[owner, image_rows]
        return remote(block, block, send_sem.at[7], c1_sem.at[owner], partner)

    def shared(owner):
        block = kvg.at[owner, pl.ds(pl.multiple_of((1 - core) * TOKENS, TOKENS), TOKENS)]
        remote(block, block, send_sem.at[7], c1_sem.at[owner], partner).wait_recv()

    def take2(*places):
        for place in places:
            for half in range(2):
                for side in both_sides:
                    if place < 8 or side == half:
                        spread2(side, place, place, half).wait_recv()
                        forward2(side, place, half)
            for side in both_sides[: 1 if place == 8 else 2]:
                share(ring(place if side else -place)).start()

    def owners_of(place):
        if place == 0:
            return (z,)
        return (ring(8),) if place == 8 else (ring(-place), ring(place))

    def copies_c2(k):
        lanes = pl.ds(0, HEAD_SIZE if k in (0, 8) else 2 * HEAD_SIZE)
        return [
            remote(
                c2_src.at[k, chip_at(n), :, lanes], c2_dst.at[k, n - 1, :, lanes],
                send_sem.at[8], c2_sem.at[k, n - 1], (chip_at(n) * 2 + core, z),
            )
            for n in range(1, CHIPS)
        ]

    def multiply(*places):
        for place in places:
            k = place
            owners = owners_of(place)
            for owner in owners:
                shared(owner)
            product = matmul(
                ft_ref[...], jnp.concatenate([kvg[n] for n in owners], 1) if len(owners) > 1 else kvg[owners[0]], ((1,), (0,))
            )
            lanes = pl.ds(0, HEAD_SIZE * len(owners))
            c2_own[k, :, lanes] = product
            c2_src[k, :, :, lanes] = product.astype(BF16).reshape(CHIPS, ROWS, -1)
            for copy in copies_c2(k):
                copy.start()

    def finish(place):
        k = place
        lanes = pl.ds(0, HEAD_SIZE * len(owners_of(k)))
        total = c2_own[k, pl.ds(pl.multiple_of(chip * ROWS, ROWS), ROWS), lanes]
        for n, copy in enumerate(copies_c2(k)):
            copy.wait_recv()
            total = total + c2_dst[k, n, :, lanes].astype(F32)
        total = (total * (1.0 / math.sqrt(CTX * TOKENS))).astype(BF16)
        for n, owner in enumerate(owners_of(place)):
            chunk = lax.rem(owner + 8, RING)
            columns = pl.ds(pl.multiple_of(chunk * HEAD_SIZE, HEAD_SIZE), HEAD_SIZE)
            wg_ref[:, columns] = total[:, n * HEAD_SIZE : (n + 1) * HEAD_SIZE]

    for half in range(2):
        total = gathered(ring(8), half)
        for side in both_sides:
            total = summed(side, 0, half, total)
        start = pl.multiple_of(core * TOKENS + half * HALF, HALF)
        kvg[z, pl.ds(start, HALF)] = total.astype(BF16)
        for side in both_sides:
            forward2(side, 0, half)
    share(z).start()
    features.wait_recv()
    take2(3, 2, 1)
    multiply(0, 3, 2, 1)
    take2(6, 5, 4)
    multiply(6, 5, 4)
    take2(8)
    multiply(8)
    take2(7)
    multiply(7)
    for place in (0, 1, 3, 2, 4, 6, 5, 7, 8):
        finish(place)
    out_w = pltpu.make_async_copy(wg_ref, wg_hbm, out_sem.at[1])
    out_w.start()

    fifteen = pl.ds(0, RING - 1)
    sent = (
        part.at[fifteen],
        ft_src.at[0],
        pg_src.at[fifteen],
        pg_src,
        pg_src,
        pg_src.at[fifteen],
        pg_src.at[fifteen],
        pg_src,
        c2_dst.at[pl.ds(0, 8)],
    )
    for n, block in enumerate(sent):
        remote(block, block, send_sem.at[n], in_sem.at[0], partner).wait_send()
    out_q.wait()
    out_w.wait()


def settle(a_in, b_in, a_out, b_out):
    a_out[...] = a_in[...]
    b_out[...] = b_in[...]


def per_device(queries, image_feats, key_value_weight, output_gradient, spans):
    anywhere = pl.BlockSpec(memory_space=pl.ANY)
    chunk = (TOKENS, HEAD_SIZE)
    double = (2 * TOKENS, HEAD_SIZE)
    dma = pltpu.SemaphoreType.DMA
    vmem = pltpu.VMEM
    results = pl.pallas_call(
        kernel,
        out_shape=(
            jax.ShapeDtypeStruct(queries.shape, BF16),
            jax.ShapeDtypeStruct((ROWS, 2048), BF16),
        ),
        in_specs=[anywhere] * 5,
        out_specs=(anywhere, anywhere),
        scratch_shapes=[
            pltpu.SMEM((2, CTX), jnp.int32),
            vmem(image_feats.shape, BF16),
            vmem(key_value_weight.shape, BF16),
            vmem(queries.shape, BF16),
            vmem(output_gradient.shape, BF16),
            vmem(queries.shape, BF16),
            vmem((ROWS, 2048), BF16),
            vmem((2, 256, TOKENS), BF16),
            vmem((256, 2 * TOKENS), BF16),
            vmem((RING, *chunk), F32),
            vmem((2, 8, *chunk), F32),
            vmem((RING, *double), BF16),
            vmem((RING, *chunk), F32),
            vmem((RING, *chunk), BF16),
            vmem((RING, *chunk), BF16),
            vmem((2, 8, *chunk), BF16),
            vmem((2, 8, *chunk), BF16),
            vmem((RING, *double), BF16),
            vmem((9, 256, 2 * HEAD_SIZE), F32),
            vmem((9, CHIPS, ROWS, 2 * HEAD_SIZE), BF16),
            vmem((9, CHIPS - 1, ROWS, 2 * HEAD_SIZE), BF16),
            dma((5,)),
            dma((2,)),
            dma((9,)),
            dma((1,)),
            dma((2, 8, 2)),
            dma((2, 8, 2)),
            dma((RING,)),
            dma((KV_HEADS,)),
            dma((2, 8, 2)),
            dma((2, 8, 2)),
            dma((RING,)),
            dma((9, CHIPS - 1)),
        ],
        compiler_params=pltpu.CompilerParams(
            collective_id=0, has_side_effects=True, vmem_limit_bytes=60 * 1024 * 1024
        ),
    )(queries, image_feats, key_value_weight, output_gradient, spans.T)
    inside = pl.BlockSpec(memory_space=pltpu.VMEM)
    return pl.pallas_call(
        settle,
        out_shape=tuple(jax.ShapeDtypeStruct(r.shape, r.dtype) for r in results),
        in_specs=[inside] * 2,
        out_specs=(inside, inside),
    )(*results)


def solution(mesh):
    return jax.shard_map(
        per_device,
        mesh=mesh,
        in_specs=(
            P(("ctx", "head"), None),
            P("ctx", "head"),
            P("head", None),
            P(("ctx", "head"), None),
            P(),
        ),
        out_specs=(P(("ctx", "head"), None), P(("head", "ctx"), None)),
        check_vma=False,
    )
```

```python
import math

import jax
import jax.numpy as jnp
from jax import lax
from jax.experimental import pallas as pl
from jax.experimental.pallas import tpu as pltpu
from jax.sharding import PartitionSpec as P

RING = 16
CTX = 32
SIDE = 4
CHIPS = SIDE * SIDE
HEAD_SIZE = 128
KV_HEADS = 8
GROUP = 8
WIDE = GROUP * HEAD_SIZE
TOKENS = 128
ROWS = 16
TEXT_PER_INDEX = 256
HALF = TOKENS // 2
NEG_FILL = -1e30
BF16 = jnp.bfloat16
F32 = jnp.float32

SPREAD = {3: 0, 2: 0, 1: 0, 6: 3, 5: 3, 4: 3, 8: 6, 7: 6}
GATHER = {3: 0, 2: 0, 1: 0, 6: 3, 5: 3, 4: 3, 8: 6, 7: 6}
PROJECT = {3: 0, 1: 0, 6: 3, 4: 3, 2: 3, 8: 6, 7: 6, 5: 6}
GATHER_INNER = (6, 3)

OTHERS = sorted(
    range(1, CHIPS), key=lambda n: -min(n // SIDE, SIDE - n // SIDE) - min(n % SIDE, SIDE - n % SIDE)
)


def children(tree, place):
    return [q for q, p in tree.items() if p == place]


def remote(src, dst, send_sem, recv_sem, device):
    return pltpu.make_async_remote_copy(
        src_ref=src,
        dst_ref=dst,
        send_sem=send_sem,
        recv_sem=recv_sem,
        device_id=device,
        device_id_type=pl.DeviceIdType.MESH,
    )


def matmul(a, b, dims):
    return lax.dot_general(a, b, (dims, ((), ())), preferred_element_type=F32)


def kernel(
    q_hbm, f_hbm, w_hbm, g_hbm, spans_hbm,
    qg_hbm, wg_hbm,
    spans, f_ref, w_ref, q_ref, g_ref, qg_ref, wg_ref, ft_src, ft_ref,
    part, r1, kv, own, pg_src, pg_dst, s2, r2, kvg,
    c2_own, c2_src, c2_dst,
    in_sem, out_sem, send_sem,
    ft_sem, r1_sem, ag1_sem, prev_sem, pg_sem, r2_sem, ag2_sem, c1_sem, c2_sem,
):
    z = lax.axis_index("head")
    ctx = lax.axis_index("ctx")
    core = lax.rem(ctx, 2)
    chip = ctx // 2
    y = lax.rem(chip, SIDE)
    x = chip // SIDE

    def ring(offset):
        return lax.rem(z + (offset + 2 * RING), RING)

    def chip_at(n):
        return lax.rem(x + n // SIDE, SIDE) * SIDE + lax.rem(y + n % SIDE, SIDE)

    later = (lax.rem(ctx + 1, CTX), z)
    earlier = (lax.rem(ctx + CTX - 1, CTX), z)
    partner = (chip * 2 + (1 - core), z)

    loads = [
        pltpu.make_async_copy(src, dst, in_sem.at[n])
        for n, (src, dst) in enumerate(
            ((f_hbm, f_ref), (w_hbm, w_ref), (q_hbm, q_ref), (g_hbm, g_ref), (spans_hbm, spans))
        )
    ]
    for load in loads:
        load.start()
    barrier = pltpu.get_barrier_semaphore()
    met = [(ctx, ring(d)) for d in (1, 2, 3, -1, -2, -3)] + [later, earlier]
    met += [(chip_at(n) * 2 + core, z) for n in range(1, CHIPS)]
    for device in met:
        pl.semaphore_signal(
            barrier, inc=1, device_id=device, device_id_type=pl.DeviceIdType.MESH
        )
    loads[0].wait()
    loads[1].wait()
    both_sides = (0, 1)
    halves = (pl.ds(0, HALF), pl.ds(HALF, HALF))

    def project(chunk):
        columns = pl.ds(pl.multiple_of(chunk * HEAD_SIZE, HEAD_SIZE), HEAD_SIZE)
        part[chunk] = matmul(f_ref[...], w_ref[:, columns], ((1,), (0,)))

    def up1(side, place, half):
        way = 1 - 2 * side
        owner = ring(-way * place)
        target = ring(-way * (place - PROJECT[place]))
        return remote(
            part.at[owner, halves[half]], r1.at[side, place - 1, halves[half]],
            send_sem.at[0], r1_sem.at[side, place - 1, half], (ctx, target),
        )

    def send1(half, *places):
        for place in places:
            for side in both_sides:
                if place < 8 or side == half:
                    up1(side, place, half).start()

    def sum1(half, place):
        for side in both_sides:
            way = 1 - 2 * side
            owner = ring(-way * place)
            for q in children(PROJECT, place):
                if q < 8 or side == half:
                    up1(side, q, half).wait_recv()
                    part[owner, halves[half]] += r1[side, q - 1, halves[half]]
            up1(side, place, half).start()

    project(ring(8))
    pl.semaphore_wait(barrier, len(met))
    send1(0, 8)
    for place in (7, 5):
        for side in both_sides:
            project(ring(place if side else -place))
        send1(0, place)
    send1(1, 8, 7, 5)
    for place in (6, 4, 2, 3, 1, 0):
        for side in both_sides:
            if place > 0 or side == 0:
                project(ring(place if side else -place))
    turned = f_ref[...].astype(F32).T.astype(BF16)
    image_lanes = pl.ds(pl.multiple_of(core * TOKENS, TOKENS), TOKENS)
    for n in range(CTX):
        ft_src[n % 2, pl.ds((n // 2) * ROWS, ROWS), :] = turned[n * ROWS : (n + 1) * ROWS]
    ft_ref[:, image_lanes] = ft_src[core]
    features = remote(
        ft_src.at[1 - core], ft_ref.at[:, image_lanes], send_sem.at[1], ft_sem.at[0], partner
    )
    features.start()
    sum1(0, 6)
    sum1(1, 6)
    send1(0, 4, 2)
    send1(1, 4, 2)
    sum1(0, 3)
    sum1(1, 3)
    send1(0, 1)
    send1(1, 1)

    own_rows, prev_rows = pl.ds(TOKENS, TOKENS), pl.ds(0, TOKENS)

    def spread1(side, place, child, half):
        way = 1 - 2 * side
        block = kv.at[ring(-way * place), pl.ds(TOKENS + half * HALF, HALF)]
        target = ring(way * (child - place))
        return remote(
            block, block, send_sem.at[2], ag1_sem.at[side, child - 1, half], (ctx, target)
        )

    def forward1(side, place, half):
        for child in children(SPREAD, place):
            if child < 8 or side == half:
                spread1(side, place, child, half).start()

    def pass_on(chunk):
        return remote(
            kv.at[chunk, own_rows], kv.at[chunk, prev_rows],
            send_sem.at[3], prev_sem.at[chunk], later,
        )

    def take1(*places):
        for place in places:
            for half in range(2):
                for side in both_sides:
                    if place < 8 or side == half:
                        spread1(side, place, place, half).wait_recv()
                        forward1(side, place, half)
            for side in both_sides[: 1 if place == 8 else 2]:
                pass_on(ring(place if side else -place)).start()

    for half in range(2):
        total = part[z, halves[half]]
        for q in children(PROJECT, 0):
            for side in both_sides:
                up1(side, q, half).wait_recv()
                total = total + r1[side, q - 1, halves[half]]
        kv[z, pl.ds(TOKENS + half * HALF, HALF)] = total.astype(BF16)
        for side in both_sides:
            forward1(side, 0, half)
    pass_on(z).start()
    loads[2].wait()
    loads[3].wait()
    loads[4].wait()

    lane = lax.broadcasted_iota(jnp.int32, (1, TOKENS), 1)
    token = ctx * TEXT_PER_INDEX + z * ROWS + lax.rem(lane, ROWS)
    before = jnp.maximum(ctx - 1, 0)
    prev_ok = (token >= spans[0, before]) & (token < spans[1, before]) & (ctx > 0)
    own_ok = (token >= spans[0, ctx]) & (token < spans[1, ctx])
    is_own = lax.broadcasted_iota(jnp.int32, (2 * TOKENS, TOKENS), 0) >= TOKENS
    allowed = (is_own & own_ok) | (jnp.logical_not(is_own) & prev_ok)
    scaling = 1.0 / math.sqrt(HEAD_SIZE)

    def stacked(ref, head):
        block = ref[:, pl.ds(pl.multiple_of(head * WIDE, WIDE), WIDE)]
        return jnp.concatenate(
            [block[:, n * HEAD_SIZE : (n + 1) * HEAD_SIZE] for n in range(GROUP)], 0
        )

    def attend(head):
        for n in range(2):
            pass_on(2 * head + n).wait_recv()
        keys, values = kv[2 * head], kv[2 * head + 1]
        query, grad = stacked(q_ref, head), stacked(g_ref, head)
        scores = matmul(keys, query, ((1,), (1,))) * scaling
        scores = jnp.where(allowed, scores, NEG_FILL)
        grad_prob = matmul(values, grad, ((1,), (1,)))
        weights = jnp.exp(scores - jnp.max(scores, 0, keepdims=True))
        probs = weights * (1.0 / jnp.sum(weights, 0, keepdims=True))
        probs = jnp.where(allowed, probs, 0.0)
        prob_low = probs.astype(BF16)
        row_dot = jnp.sum(prob_low.astype(F32) * grad_prob, 0, keepdims=True)
        score_low = (probs * (grad_prob - row_dot)).astype(BF16)
        key_grad = matmul(score_low, query, ((1,), (0,))) * scaling
        value_grad = matmul(prob_low, grad, ((1,), (0,)))
        pg_src[2 * head] = key_grad[:TOKENS].astype(BF16)
        pg_src[2 * head + 1] = value_grad[:TOKENS].astype(BF16)
        send_back(head).start()
        own[2 * head] = key_grad[TOKENS:]
        own[2 * head + 1] = value_grad[TOKENS:]
        query_grad = (matmul(score_low, keys, ((0,), (0,))) * scaling).astype(BF16)
        qg_ref[:, pl.ds(pl.multiple_of(head * WIDE, WIDE), WIDE)] = jnp.concatenate(
            [query_grad[n * ROWS : (n + 1) * ROWS] for n in range(GROUP)], 1
        )

    def send_back(head):
        pair = pl.ds(2 * head, 2)
        return remote(
            pg_src.at[pair], pg_dst.at[pair], send_sem.at[4], pg_sem.at[head], earlier
        )

    turn = 2 * lax.rem(z, 2) - 1

    def head_at(k):
        offset = ((k + 1) // 2) * (1 if k % 2 else -1)
        return lax.rem(z // 2 + turn * offset + KV_HEADS, KV_HEADS)

    def up2(side, place, half):
        way = 1 - 2 * side
        target = ring(-way * (place - GATHER[place]))
        return remote(
            s2.at[side, place - 1, halves[half]], r2.at[side, place - 1, halves[half]],
            send_sem.at[5], r2_sem.at[side, place - 1, half], (ctx, target),
        )

    def gathered(chunk, half):
        return own[chunk, halves[half]] + pg_dst[chunk, halves[half]].astype(F32)

    def summed(side, place, half, total):
        for q in children(GATHER, place):
            if q < 8 or side == half:
                up2(side, q, half).wait_recv()
                total = total + r2[side, q - 1, halves[half]].astype(F32)
        return total

    def send2(place):
        for half in range(2):
            for side in both_sides:
                if place < 8 or side == half:
                    way = 1 - 2 * side
                    total = summed(side, place, half, gathered(ring(8 - way * place), half))
                    s2[side, place - 1, halves[half]] = total.astype(BF16)
                    up2(side, place, half).start()

    def leaf2(k):
        send_back(head_at(k)).wait_recv()
        if 8 - k not in GATHER_INNER:
            send2(8 - k)

    take1(1, 3, 2)
    for k in (0, 1, 2):
        attend(head_at(k))
    take1(6, 5, 4)
    for k in (0, 1, 2):
        leaf2(k)
    for k in (3, 4, 5):
        attend(head_at(k))
    take1(7, 8)
    send2(6)
    for k in (3, 4):
        leaf2(k)
    for k in (6, 7):
        attend(head_at(k))
    out_q = pltpu.make_async_copy(qg_ref, qg_hbm, out_sem.at[0])
    out_q.start()
    for k in (5, 6, 7):
        leaf2(k)
    send2(3)
    image_rows = pl.ds(pl.multiple_of(core * TOKENS, TOKENS), TOKENS)

    def spread2(side, place, child, half):
        way = 1 - 2 * side
        start = pl.multiple_of(core * TOKENS + half * HALF, HALF)
        block = kvg.at[ring(-way * place), pl.ds(start, HALF)]
        target = ring(way * (child - place))
        return remote(
            block, block, send_sem.at[6], ag2_sem.at[side, child - 1, half], (ctx, target)
        )

    def forward2(side, place, half):
        for child in children(SPREAD, place):
            if child < 8 or side == half:
                spread2(side, place, child, half).start()

    def share(owner):
        block = kvg.at[owner, image_rows]
        return remote(block, block, send_sem.at[7], c1_sem.at[owner], partner)

    def shared(owner):
        block = kvg.at[owner, pl.ds(pl.multiple_of((1 - core) * TOKENS, TOKENS), TOKENS)]
        remote(block, block, send_sem.at[7], c1_sem.at[owner], partner).wait_recv()

    def take2(*places):
        for place in places:
            for half in range(2):
                for side in both_sides:
                    if place < 8 or side == half:
                        spread2(side, place, place, half).wait_recv()
                        forward2(side, place, half)
            for side in both_sides[: 1 if place == 8 else 2]:
                share(ring(place if side else -place)).start()

    def owners_of(place):
        if place == 0:
            return (z,)
        return (ring(8),) if place == 8 else (ring(-place), ring(place))

    def copies_c2(k):
        lanes = pl.ds(0, HEAD_SIZE if k in (0, 8) else 2 * HEAD_SIZE)
        return [
            remote(
                c2_src.at[k, chip_at(n), :, lanes], c2_dst.at[k, n - 1, :, lanes],
                send_sem.at[8], c2_sem.at[k, n - 1], (chip_at(n) * 2 + core, z),
            )
            for n in OTHERS
        ]

    def multiply(*places):
        for place in places:
            k = place
            owners = owners_of(place)
            for owner in owners:
                shared(owner)
            product = matmul(
                ft_ref[...], jnp.concatenate([kvg[n] for n in owners], 1) if len(owners) > 1 else kvg[owners[0]], ((1,), (0,))
            )
            lanes = pl.ds(0, HEAD_SIZE * len(owners))
            c2_own[k, :, lanes] = product
            c2_src[k, :, :, lanes] = product.astype(BF16).reshape(CHIPS, ROWS, -1)
            for copy in copies_c2(k):
                copy.start()

    def finish(place):
        k = place
        lanes = pl.ds(0, HEAD_SIZE * len(owners_of(k)))
        total = c2_own[k, pl.ds(pl.multiple_of(chip * ROWS, ROWS), ROWS), lanes]
        for n, copy in zip(OTHERS, copies_c2(k)):
            copy.wait_recv()
            total = total + c2_dst[k, n - 1, :, lanes].astype(F32)
        total = (total * (1.0 / math.sqrt(CTX * TOKENS))).astype(BF16)
        for n, owner in enumerate(owners_of(place)):
            chunk = lax.rem(owner + 8, RING)
            columns = pl.ds(pl.multiple_of(chunk * HEAD_SIZE, HEAD_SIZE), HEAD_SIZE)
            wg_ref[:, columns] = total[:, n * HEAD_SIZE : (n + 1) * HEAD_SIZE]

    for half in range(2):
        total = gathered(ring(8), half)
        for side in both_sides:
            total = summed(side, 0, half, total)
        start = pl.multiple_of(core * TOKENS + half * HALF, HALF)
        kvg[z, pl.ds(start, HALF)] = total.astype(BF16)
        for side in both_sides:
            forward2(side, 0, half)
    share(z).start()
    features.wait_recv()
    take2(3, 2, 1)
    multiply(0, 3, 2, 1)
    take2(6, 5, 4)
    multiply(6, 5, 4)
    take2(8)
    multiply(8)
    take2(7)
    multiply(7)
    for place in (0, 1, 3, 2, 4, 6, 5, 7, 8):
        finish(place)
    out_w = pltpu.make_async_copy(wg_ref, wg_hbm, out_sem.at[1])
    out_w.start()

    fifteen = pl.ds(0, RING - 1)
    sent = (
        part.at[fifteen],
        ft_src.at[0],
        pg_src.at[fifteen],
        pg_src,
        pg_src,
        pg_src.at[fifteen],
        pg_src.at[fifteen],
        pg_src,
        c2_dst.at[pl.ds(0, 8)],
    )
    for n, block in enumerate(sent):
        remote(block, block, send_sem.at[n], in_sem.at[0], partner).wait_send()
    out_q.wait()
    out_w.wait()


def settle(a_in, b_in, a_out, b_out):
    a_out[...] = a_in[...]
    b_out[...] = b_in[...]


def per_device(queries, image_feats, key_value_weight, output_gradient, spans):
    anywhere = pl.BlockSpec(memory_space=pl.ANY)
    chunk = (TOKENS, HEAD_SIZE)
    double = (2 * TOKENS, HEAD_SIZE)
    dma = pltpu.SemaphoreType.DMA
    vmem = pltpu.VMEM
    results = pl.pallas_call(
        kernel,
        out_shape=(
            jax.ShapeDtypeStruct(queries.shape, BF16),
            jax.ShapeDtypeStruct((ROWS, 2048), BF16),
        ),
        in_specs=[anywhere] * 5,
        out_specs=(anywhere, anywhere),
        scratch_shapes=[
            pltpu.SMEM((2, CTX), jnp.int32),
            vmem(image_feats.shape, BF16),
            vmem(key_value_weight.shape, BF16),
            vmem(queries.shape, BF16),
            vmem(output_gradient.shape, BF16),
            vmem(queries.shape, BF16),
            vmem((ROWS, 2048), BF16),
            vmem((2, 256, TOKENS), BF16),
            vmem((256, 2 * TOKENS), BF16),
            vmem((RING, *chunk), F32),
            vmem((2, 8, *chunk), F32),
            vmem((RING, *double), BF16),
            vmem((RING, *chunk), F32),
            vmem((RING, *chunk), BF16),
            vmem((RING, *chunk), BF16),
            vmem((2, 8, *chunk), BF16),
            vmem((2, 8, *chunk), BF16),
            vmem((RING, *double), BF16),
            vmem((9, 256, 2 * HEAD_SIZE), F32),
            vmem((9, CHIPS, ROWS, 2 * HEAD_SIZE), BF16),
            vmem((9, CHIPS - 1, ROWS, 2 * HEAD_SIZE), BF16),
            dma((5,)),
            dma((2,)),
            dma((9,)),
            dma((1,)),
            dma((2, 8, 2)),
            dma((2, 8, 2)),
            dma((RING,)),
            dma((KV_HEADS,)),
            dma((2, 8, 2)),
            dma((2, 8, 2)),
            dma((RING,)),
            dma((9, CHIPS - 1)),
        ],
        compiler_params=pltpu.CompilerParams(
            collective_id=0, has_side_effects=True, vmem_limit_bytes=60 * 1024 * 1024
        ),
    )(queries, image_feats, key_value_weight, output_gradient, spans.T)
    inside = pl.BlockSpec(memory_space=pltpu.VMEM)
    return pl.pallas_call(
        settle,
        out_shape=tuple(jax.ShapeDtypeStruct(r.shape, r.dtype) for r in results),
        in_specs=[inside] * 2,
        out_specs=(inside, inside),
    )(*results)


def solution(mesh):
    return jax.shard_map(
        per_device,
        mesh=mesh,
        in_specs=(
            P(("ctx", "head"), None),
            P("ctx", "head"),
            P("head", None),
            P(("ctx", "head"), None),
            P(),
        ),
        out_specs=(P(("ctx", "head"), None), P(("head", "ctx"), None)),
        check_vma=False,
    )
```
